512 devices in a mesh: seq: 64 (over x, z, core), tensor: 8 (over y).
Axes of the slice: x: 4, y: 8, z: 8, core: 2. Of those that a mesh axis runs over, the one named last changes fastest.
Arguments:
- signal: bfloat16 [16384, 4096], P('seq', 'tensor'), may hold values from -6 to 6
- kernel_taps: float32 [16384, 4096], P('seq', 'tensor'), may hold values from -3 to 3
- gating: bfloat16 [16384, 4096], P('seq', 'tensor'), may hold values from -6 to 6
- skip_gain: float32 [4096], P('tensor'), may hold values from 0.5 to 1.5
- out_weight: bfloat16 [4096, 4096], P('seq', 'tensor'), may hold values from -0.09375 to 0.09375
Outputs:
- projected: bfloat16 [16384, 4096], P('seq', 'tensor')
The draws below stay inside these ranges and needn't reach their ends.
All inputs are finite; a program needn't handle non-finite values.
Results may differ from the reference program's by a relative error of at most 0.0049.
Values may be sent and summed in bfloat16 or wider, within the bound.
No kernel may reach another device: no remote copies, remote signals or barrier semaphores. Data moves between devices by JAX's collectives and lax.ppermute only.
A program may use at most 64 MiB of HBM per device.

```python
import jax
import jax.numpy as jnp

SLAB_CHANNELS = 4096
D = 4096
TOKEN_LENGTH = 16384
FFT_LEN = 32768


def unit_scaling(rate):
    return jnp.sqrt((1.0 - jnp.exp(-2.0 * rate)) / (1.0 - jnp.exp(-2.0 * rate * TOKEN_LENGTH)))


def draw_kernel_taps(key, part):
    key = jax.random.fold_in(key, 11)
    derived_random_keys = jax.random.split(key, 8)
    shape = (TOKEN_LENGTH, SLAB_CHANNELS)
    rough_slow = jax.random.normal(derived_random_keys[0], shape)
    rough_fast = jax.random.normal(derived_random_keys[6], shape)
    slow_energy = jax.random.uniform(derived_random_keys[1], (SLAB_CHANNELS,), minval=0.3, maxval=0.6)
    slow_rate = jax.random.uniform(derived_random_keys[2], (SLAB_CHANNELS,), minval=0.2, maxval=1.5) / TOKEN_LENGTH
    fast_rate = jax.random.uniform(derived_random_keys[3], (SLAB_CHANNELS,), minval=1.0 / 60.0, maxval=1.0 / 25.0)
    channel_gain = jnp.exp(jax.random.uniform(derived_random_keys[7], (SLAB_CHANNELS,), minval=jnp.log(0.7), maxval=jnp.log(2.1)))
    nucleotide_offsets = jnp.arange(TOKEN_LENGTH, dtype=jnp.float32)[:, None]
    spike_positions = jax.random.randint(derived_random_keys[4], (3,), 1, TOKEN_LENGTH)
    spike_retained = jax.random.uniform(derived_random_keys[5], (3, SLAB_CHANNELS), minval=0.5, maxval=0.8)
    logarithmic_decay = jnp.zeros(shape, jnp.float32)
    for spike_count in range(3):
        accepted_flags = (nucleotide_offsets >= spike_positions[spike_count].astype(jnp.float32)).astype(jnp.float32)
        logarithmic_decay = logarithmic_decay + accepted_flags * jnp.log(spike_retained[spike_count])[None, :]
    slow_part = rough_slow * jnp.exp(-slow_rate[None, :] * nucleotide_offsets + logarithmic_decay) * unit_scaling(slow_rate)[None, :]
    fast_part = rough_fast * jnp.exp(-fast_rate[None, :] * nucleotide_offsets) * unit_scaling(fast_rate)[None, :]
    mixed = jnp.sqrt(slow_energy)[None, :] * slow_part + jnp.sqrt(1.0 - slow_energy)[None, :] * fast_part
    return jnp.clip(channel_gain[None, :] * mixed, -3.0, 3.0)


def level_of(key, extent, cuts, smallest, largest):
    def one(dim, parts):
        steps = jax.random.uniform(jax.random.fold_in(jax.random.fold_in(key, 6), dim), (parts,), jnp.float32, smallest / len(cuts), largest / len(cuts))
        return jnp.repeat(jnp.exp(steps), extent[dim] // parts).reshape((-1,) + (1,) * (len(extent) - dim - 1))

    gain = one(*cuts[0])
    for cut in cuts[1:]:
        gain = gain * one(*cut)
    return gain


def noise(rng, dims, width, bound, cuts=(), held_as=jnp.bfloat16):
    drawn = jax.random.normal(rng, dims, jnp.float32) * width
    if len(cuts) > 0:
        drawn = level_of(rng, dims, cuts, -0.22, 0.18) * drawn
    return jnp.clip(drawn, min=-bound, max=bound).astype(held_as)


def setup_inputs(seed: int = 0) -> dict:
    splits = jax.random.split(jax.random.key(seed), 6)
    signal = noise(splits[0], (TOKEN_LENGTH, SLAB_CHANNELS), 1.0, 6.0, ((0, 64), (1, 8)))
    kernel_taps = draw_kernel_taps(jax.random.fold_in(splits[5], 71), 0)
    gating = noise(splits[2], (TOKEN_LENGTH, SLAB_CHANNELS), 1.0, 6.0, ((0, 64), (1, 8)))
    skip_gain = jnp.clip(0.5 + 1.0 * jax.random.uniform(splits[3], (SLAB_CHANNELS,), jnp.float32) ** level_of(splits[3], (SLAB_CHANNELS,), ((0, 8),), -0.2, 0.2), 0.5, 1.5)
    out_weight = noise(splits[4], (SLAB_CHANNELS, D), SLAB_CHANNELS ** -0.5, 0.09375, ((0, 64), (1, 8)))
    return dict(signal=signal, kernel_taps=kernel_taps, gating=gating, skip_gain=skip_gain, out_weight=out_weight)


def reference(signal, kernel_taps, gating, skip_gain, out_weight):
    values = signal.astype(jnp.float32)
    spec_sig = jnp.fft.rfft(values, n=FFT_LEN, axis=0)
    spec_ker = jnp.fft.rfft(kernel_taps, n=FFT_LEN, axis=0)
    convolved = jnp.fft.irfft(spec_sig * spec_ker, n=FFT_LEN, axis=0)[:TOKEN_LENGTH]
    gated_mix = (gating.astype(jnp.float32) * (convolved + skip_gain[None, :] * values)).astype(jnp.bfloat16)
    return jnp.dot(gated_mix, out_weight, preferred_element_type=jnp.float32).astype(jnp.bfloat16)
```

```python
import math

import jax
import jax.numpy as jnp
import ml_dtypes
import numpy as np
from jax import lax
from jax.experimental import pallas as pl
from jax.experimental.pallas import tpu as pltpu
from jax.sharding import PartitionSpec as P

F32 = jnp.float32
BF16 = jnp.bfloat16
MIB = 1024 * 1024


def split_np(table):
    high = table.astype(ml_dtypes.bfloat16)
    low = (table - high.astype(np.float64)).astype(ml_dtypes.bfloat16)
    return high, low


def phases(left, right, modulus):
    return (left[:, None] * right[None, :] % modulus) * (2.0 * math.pi / modulus)


def dft_tables(blocks, inner):
    outer = 2 * blocks
    length = outer * inner
    freqs = blocks + 1
    held = -(-freqs // 8) * 8
    f = np.arange(freqs)
    b = np.arange(blocks)
    i = np.arange(inner)
    first = np.zeros((2 * held, blocks))
    angle = phases(f, b, outer)
    first[:freqs] = np.cos(angle)
    first[held : held + freqs] = -np.sin(angle)
    first = np.concatenate(split_np(first), axis=1)
    turn = np.zeros((2, held, inner), np.float32)
    turn[0, :freqs] = np.cos(phases(f, i, length))
    turn[1, :freqs] = np.sin(phases(f, i, length))
    angle = phases(i, i, inner)
    cos, sin = np.cos(angle), np.sin(angle)
    mid_high, mid_low = split_np(np.block([[cos, -sin], [sin, cos]]))
    mid = np.concatenate([mid_high, mid_high, mid_low], axis=0)
    weight = np.where((f == 0) | (f == blocks), 1.0, 2.0) / length
    last = np.zeros((blocks, 2 * held))
    angle = phases(b, f, outer)
    last[:, :freqs] = np.cos(angle) * weight
    last[:, held : held + freqs] = -np.sin(angle) * weight
    last_high, last_low = split_np(last)
    last = np.concatenate([last_high, last_high, last_low], axis=1)
    return first, turn, mid, last


def split(values):
    high = values.astype(BF16)
    low = (values - high.astype(F32)).astype(BF16)
    return high, low


def pack_kernel(signal_ref, taps_ref, *refs):
    tables, (out_ref, *kept), (signal, taps, arrived) = refs[:4], refs[4:9], refs[9:]
    moves = [(signal_ref, signal), (taps_ref, taps), *zip(tables, kept)]
    copies = [pltpu.make_async_copy(src, dst, arrived.at[n]) for n, (src, dst) in enumerate(moves)]
    for copy in copies:
        copy.start()
    tokens, channels = signal.shape
    copies[0].wait()
    sig = signal[...].astype(F32).T.reshape(channels // 8, 8, tokens)
    copies[1].wait()
    ker = taps[...].T.reshape(channels // 8, 8, tokens)
    out_ref[...] = jnp.concatenate([sig, ker], axis=1).astype(BF16)
    for copy in copies[2:]:
        copy.wait()


def conv_kernel(x_ref, first_ref, turn_ref, mid_ref, last_ref, out_ref, flat, cat, spec, back):
    blocks, rows, inner = x_ref.shape
    chans = rows // 2
    held = turn_ref.shape[1]
    lanes = flat.shape[1]
    halves = inner // lanes
    span = blocks * rows
    for h in range(halves):
        flat[h * span : (h + 1) * span, :] = (
            x_ref[:, :, h * lanes : (h + 1) * lanes].astype(F32).reshape(span, lanes)
        )
    for c in range(chans):
        parts = []
        for row in (c, chans + c):
            x = jnp.concatenate(
                [flat[pl.ds(h * span + row, blocks, stride=rows), :] for h in range(halves)], axis=1
            ).astype(BF16)
            a = jnp.dot(first_ref[...], jnp.concatenate([x, x], axis=0), preferred_element_type=F32)
            real, imag = a[:held], a[held:]
            parts.append(
                jnp.concatenate(
                    [real * turn_ref[0] + imag * turn_ref[1], imag * turn_ref[0] - real * turn_ref[1]], axis=1
                )
            )
        high, low = split(jnp.concatenate(parts, axis=0))
        here = pl.ds(c * 2 * held, 2 * held)
        cat[here, : 2 * inner] = high
        cat[here, 2 * inner : 4 * inner] = low
        cat[here, 4 * inner :] = high
    spec[...] = jnp.dot(cat[...], mid_ref[...], preferred_element_type=F32)
    for c in range(0, chans, 2):
        parts = []
        for one in (c, c + 1):
            s = spec[pl.ds(one * 2 * held, held), :]
            k = spec[pl.ds(one * 2 * held + held, held), :]
            sr, si, kr, ki = s[:, :inner], s[:, inner:], k[:, :inner], k[:, inner:]
            parts.append(jnp.concatenate([sr * kr - si * ki, -(sr * ki + si * kr)], axis=1))
        high, low = split(jnp.concatenate(parts, axis=0))
        here = pl.ds(c * held, 2 * held)
        cat[here, : 2 * inner] = high
        cat[here, 2 * inner : 4 * inner] = low
        cat[here, 4 * inner :] = high
    half = chans * held
    spec[:half, :] = jnp.dot(cat[:half, :], mid_ref[...], preferred_element_type=F32)
    for c in range(chans):
        q = spec[pl.ds(c * held, held), :]
        qr, qi = q[:, :inner], -q[:, inner:]
        v = jnp.concatenate(
            [qr * turn_ref[0] - qi * turn_ref[1], qr * turn_ref[1] + qi * turn_ref[0]], axis=0
        )
        high, low = split(v)
        y = jnp.dot(last_ref[...], jnp.concatenate([high, low, high], axis=0), preferred_element_type=F32)
        for h in range(inner // lanes):
            back[pl.ds(h * chans + c, blocks, stride=rows), :] = y[:, h * lanes : (h + 1) * lanes]
    out_ref[...] = back[...].reshape(blocks, rows, lanes).astype(BF16)


def gate_kernel(back_ref, signal_ref, gating_ref, skip_ref, out_ref):
    groups, rows, lanes = back_ref.shape
    chans = 8
    tokens, channels = signal_ref.shape
    y = back_ref[...].astype(F32)
    for h in range(tokens // lanes):
        conv = y[:, h * chans : (h + 1) * chans, :].reshape(channels, lanes).T
        here = pl.ds(h * lanes, lanes)
        mixed = conv + skip_ref[...] * signal_ref[here, :].astype(F32)
        out_ref[here, :] = (gating_ref[here, :].astype(F32) * mixed).astype(BF16)


def project_kernel(index_ref, *refs):
    *pieces, w_ref, total_ref, last_ref, held, arrived = refs
    depth = held.shape[1]
    copies = []
    for n in range(len(pieces) + 1):
        rows = pl.ds(pl.multiple_of(index_ref[n] * depth, depth), depth)
        target = held.at[n] if n < len(pieces) else last_ref
        copies.append(pltpu.make_async_copy(w_ref.at[rows, :], target, arrived.at[n]))
        copies[n].start()
    total = None
    for n, piece in enumerate(pieces):
        copies[n].wait()
        product = jnp.dot(piece[...], held[n], preferred_element_type=F32)
        total = product if total is None else total + product
    total_ref[...] = total
    copies[-1].wait()


def finish_kernel(total_ref, up_ref, down_ref, w_ref, out_ref):
    piece = jnp.concatenate([up_ref[...], down_ref[...]], axis=0)
    product = jnp.dot(piece, w_ref[...], preferred_element_type=F32)
    out_ref[...] = (total_ref[...] + product).astype(BF16)


def vmem_limit(mebibytes):
    return pltpu.CompilerParams(vmem_limit_bytes=mebibytes * MIB)


def body(signal, kernel_taps, gating, skip_gain, out_weight):
    seq_count = lax.axis_size("seq")
    ring = lax.axis_size("tensor")
    tokens, channels = signal.shape
    full_weight = lax.all_gather(out_weight, "seq", axis=0, tiled=True)
    tables = [jnp.asarray(table) for table in dft_tables(seq_count, tokens)]
    vmem = pl.BlockSpec(memory_space=pltpu.VMEM)
    anywhere = pl.BlockSpec(memory_space=pl.ANY)
    packed, *tables = pl.pallas_call(
        pack_kernel,
        in_specs=[anywhere] * 6,
        out_specs=[vmem] * 5,
        out_shape=[jax.ShapeDtypeStruct((channels // 8, 16, tokens), BF16)]
        + [jax.ShapeDtypeStruct(table.shape, table.dtype) for table in tables],
        scratch_shapes=[
            pltpu.VMEM((tokens, channels), BF16),
            pltpu.VMEM((tokens, channels), F32),
            pltpu.SemaphoreType.DMA((6,)),
        ],
        compiler_params=vmem_limit(48),
    )(signal, kernel_taps, *tables)
    spread = lax.all_to_all(packed, "seq", split_axis=0, concat_axis=0, tiled=True)
    held = tables[1].shape[1]
    convolved = pl.pallas_call(
        conv_kernel,
        out_shape=jax.ShapeDtypeStruct((seq_count, 16, 128), BF16),
        scratch_shapes=[
            pltpu.VMEM((tokens // 128 * seq_count * 16, 128), F32),
            pltpu.VMEM((16 * held, 6 * tokens), BF16),
            pltpu.VMEM((16 * held, 2 * tokens), F32),
            pltpu.VMEM((seq_count * 16, 128), F32),
        ],
        compiler_params=vmem_limit(24),
    )(spread, *tables)
    returned = lax.all_to_all(convolved, "seq", split_axis=0, concat_axis=0, tiled=True)
    gated = pl.pallas_call(
        gate_kernel, out_shape=jax.ShapeDtypeStruct((tokens, channels), BF16), compiler_params=vmem_limit(8)
    )(returned, signal, gating, skip_gain.reshape(1, channels))
    up_pairs = [(t, (t + 1) % ring) for t in range(ring)]
    down_pairs = [(t, (t - 1) % ring) for t in range(ring)]
    pieces, offsets = [gated], [0]
    up = down = gated
    for n in range(1, ring // 2):
        up = lax.ppermute(up, "tensor", up_pairs)
        down = lax.ppermute(down, "tensor", down_pairs)
        pieces += [up, down]
        offsets += [-n, n]
    up = lax.ppermute(up[: tokens // 2], "tensor", up_pairs)
    down = lax.ppermute(down[tokens // 2 :], "tensor", down_pairs)
    offsets.append(ring // 2)
    index = (lax.axis_index("tensor") + jnp.asarray(offsets, jnp.int32)) % ring
    total, last_weight = pl.pallas_call(
        project_kernel,
        in_specs=[pl.BlockSpec(memory_space=pltpu.SMEM)] + [vmem] * len(pieces) + [anywhere],
        out_specs=[vmem] * 2,
        out_shape=[
            jax.ShapeDtypeStruct((tokens, channels), F32),
            jax.ShapeDtypeStruct((channels, channels), BF16),
        ],
        scratch_shapes=[
            pltpu.VMEM((len(pieces), channels, channels), BF16),
            pltpu.SemaphoreType.DMA((ring,)),
        ],
        compiler_params=vmem_limit(48),
    )(index, *pieces, full_weight)
    return pl.pallas_call(
        finish_kernel, out_shape=jax.ShapeDtypeStruct((tokens, channels), BF16), compiler_params=vmem_limit(8)
    )(total, up, down, last_weight)


def solution(mesh):
    placed = (
        P("seq", "tensor"),
        P("seq", "tensor"),
        P("seq", "tensor"),
        P("tensor"),
        P("seq", "tensor"),
    )
    return jax.shard_map(
        body, mesh=mesh, in_specs=placed, out_specs=P("seq", "tensor"), check_vma=False
    )
```

```python
import functools
import math

import jax
import jax.numpy as jnp
import ml_dtypes
import numpy as np
from jax import lax
from jax.experimental import pallas as pl
from jax.experimental.pallas import tpu as pltpu
from jax.sharding import PartitionSpec as P

F32 = jnp.float32
BF16 = jnp.bfloat16
MIB = 1024 * 1024


def split_np(table):
    high = table.astype(ml_dtypes.bfloat16)
    low = (table - high.astype(np.float64)).astype(ml_dtypes.bfloat16)
    return high, low


def phases(left, right, modulus):
    return (left[:, None] * right[None, :] % modulus) * (2.0 * math.pi / modulus)


def dft_tables(blocks, inner):
    outer = 2 * blocks
    length = outer * inner
    freqs = blocks + 1
    held = -(-freqs // 8) * 8
    f = np.arange(freqs)
    b = np.arange(blocks)
    i = np.arange(inner)
    first = np.zeros((2 * held, blocks))
    angle = phases(f, b, outer)
    first[:freqs] = np.cos(angle)
    first[held : held + freqs] = -np.sin(angle)
    turn = np.zeros((2 * held, inner))
    turn[:freqs] = np.cos(phases(f, i, length))
    turn[held : held + freqs] = np.sin(phases(f, i, length))
    angle = phases(i, i, inner)
    mid = np.concatenate([np.cos(angle), np.sin(angle)], axis=1)
    weight = np.where((f == 0) | (f == blocks), 1.0, 2.0) / length
    last = np.zeros((blocks, 2 * held))
    angle = phases(b, f, outer)
    last[:, :freqs] = np.cos(angle) * weight
    last[:, held : held + freqs] = -np.sin(angle) * weight
    last_high, last_low = split_np(last)
    parts = [
        np.concatenate(split_np(mid), axis=0),
        np.concatenate(split_np(turn), axis=1),
        np.concatenate(split_np(first), axis=1),
        np.concatenate([last_high, last_high, last_low], axis=1),
    ]
    width = 2 * inner
    table = np.concatenate([np.pad(part, ((0, 0), (0, width - part.shape[1]))) for part in parts], axis=0)
    ends = np.cumsum([part.shape[0] for part in parts])
    return table, [(int(end) - part.shape[0], int(end), part.shape[1]) for end, part in zip(ends, parts)]


def split(values):
    high = values.astype(BF16)
    low = (values - high.astype(F32)).astype(BF16)
    return high, low


def pack_kernel(signal_ref, taps_ref, out_ref):
    tokens, channels = signal_ref.shape
    sig = signal_ref[...].astype(F32).T.reshape(channels // 8, 8, tokens)
    ker = taps_ref[...].T.reshape(channels // 8, 8, tokens)
    out_ref[...] = jnp.concatenate([sig, ker], axis=1).astype(BF16)


def spread_mid(short, mid):
    inner = short.shape[1] // 2
    for n, rows in enumerate((0, 0, inner)):
        cos, sin = short[rows : rows + inner, :inner], short[rows : rows + inner, inner:]
        mid[2 * n * inner : (2 * n + 1) * inner, :inner] = cos
        mid[2 * n * inner : (2 * n + 1) * inner, inner:] = -sin
        mid[(2 * n + 1) * inner : (2 * n + 2) * inner, :inner] = sin
        mid[(2 * n + 1) * inner : (2 * n + 2) * inner, inner:] = cos


def conv_kernel(places, x_ref, table_ref, out_ref, flat, cat, spec, back, mid, turn):
    parts = [table_ref.at[pl.ds(start, end - start), pl.ds(0, width)] for start, end, width in places]
    short_ref, turn_ref, first_ref, last_ref = parts
    held = turn.shape[0] // 2
    spread_mid(short_ref, mid)
    turn[...] = turn_ref[:, : turn.shape[1]].astype(F32) + turn_ref[:, turn.shape[1] :].astype(F32)
    cos_ref, sin_ref = turn.at[pl.ds(0, held)], turn.at[pl.ds(held, held)]
    blocks, rows, inner = x_ref.shape
    chans = rows // 2
    lanes = flat.shape[1]
    halves = inner // lanes
    span = blocks * rows
    for h in range(halves):
        flat[h * span : (h + 1) * span, :] = (
            x_ref[:, :, h * lanes : (h + 1) * lanes].astype(F32).reshape(span, lanes)
        )
    for c in range(chans):
        parts = []
        for row in (c, chans + c):
            x = jnp.concatenate(
                [flat[pl.ds(h * span + row, blocks, stride=rows), :] for h in range(halves)], axis=1
            ).astype(BF16)
            a = jnp.dot(first_ref[...], jnp.concatenate([x, x], axis=0), preferred_element_type=F32)
            real, imag = a[:held], a[held:]
            parts.append(
                jnp.concatenate(
                    [real * cos_ref[...] + imag * sin_ref[...], imag * cos_ref[...] - real * sin_ref[...]], axis=1
                )
            )
        high, low = split(jnp.concatenate(parts, axis=0))
        here = pl.ds(c * 2 * held, 2 * held)
        cat[here, : 2 * inner] = high
        cat[here, 2 * inner : 4 * inner] = low
        cat[here, 4 * inner :] = high
    spec[...] = jnp.dot(cat[...], mid[...], preferred_element_type=F32)
    for c in range(0, chans, 2):
        parts = []
        for one in (c, c + 1):
            s = spec[pl.ds(one * 2 * held, held), :]
            k = spec[pl.ds(one * 2 * held + held, held), :]
            sr, si, kr, ki = s[:, :inner], s[:, inner:], k[:, :inner], k[:, inner:]
            parts.append(jnp.concatenate([sr * kr - si * ki, -(sr * ki + si * kr)], axis=1))
        high, low = split(jnp.concatenate(parts, axis=0))
        here = pl.ds(c * held, 2 * held)
        cat[here, : 2 * inner] = high
        cat[here, 2 * inner : 4 * inner] = low
        cat[here, 4 * inner :] = high
    half = chans * held
    spec[:half, :] = jnp.dot(cat[:half, :], mid[...], preferred_element_type=F32)
    for c in range(chans):
        q = spec[pl.ds(c * held, held), :]
        qr, qi = q[:, :inner], -q[:, inner:]
        v = jnp.concatenate(
            [qr * cos_ref[...] - qi * sin_ref[...], qr * sin_ref[...] + qi * cos_ref[...]], axis=0
        )
        high, low = split(v)
        y = jnp.dot(last_ref[...], jnp.concatenate([high, low, high], axis=0), preferred_element_type=F32)
        for h in range(inner // lanes):
            back[pl.ds(h * chans + c, blocks, stride=rows), :] = y[:, h * lanes : (h + 1) * lanes]
    out_ref[...] = back[...].reshape(blocks, rows, lanes).astype(BF16)


def gate_kernel(back_ref, signal_ref, gating_ref, skip_ref, out_ref):
    groups, rows, lanes = back_ref.shape
    chans = 8
    tokens, channels = signal_ref.shape
    y = back_ref[...].astype(F32)
    for h in range(tokens // lanes):
        conv = y[:, h * chans : (h + 1) * chans, :].reshape(channels, lanes).T
        here = pl.ds(h * lanes, lanes)
        mixed = conv + skip_ref[...] * signal_ref[here, :].astype(F32)
        out_ref[here, :] = (gating_ref[here, :].astype(F32) * mixed).astype(BF16)


def project_kernel(index_ref, *refs):
    *pieces, w_ref, total_ref, last_ref, held, arrived = refs
    depth = held.shape[1]
    copies = []
    for n in range(len(pieces) + 1):
        rows = pl.ds(pl.multiple_of(index_ref[n] * depth, depth), depth)
        target = held.at[n] if n < len(pieces) else last_ref
        copies.append(pltpu.make_async_copy(w_ref.at[rows, :], target, arrived.at[n]))
        copies[n].start()
    total = None
    for n, piece in enumerate(pieces):
        copies[n].wait()
        product = jnp.dot(piece[...], held[n], preferred_element_type=F32)
        total = product if total is None else total + product
    total_ref[...] = total
    copies[-1].wait()


def finish_kernel(total_ref, up_ref, down_ref, w_ref, out_ref):
    piece = jnp.concatenate([up_ref[...], down_ref[...]], axis=0)
    product = jnp.dot(piece, w_ref[...], preferred_element_type=F32)
    out_ref[...] = (total_ref[...] + product).astype(BF16)


def vmem_limit(mebibytes):
    return pltpu.CompilerParams(vmem_limit_bytes=mebibytes * MIB)


def body(signal, kernel_taps, gating, skip_gain, out_weight):
    seq_count = lax.axis_size("seq")
    ring = lax.axis_size("tensor")
    tokens, channels = signal.shape
    full_weight = lax.all_gather(out_weight, "seq", axis=0, tiled=True)
    table, places = dft_tables(seq_count, tokens)
    turn_rows = places[1][1] - places[1][0]
    held = turn_rows // 2
    vmem = pl.BlockSpec(memory_space=pltpu.VMEM)
    packed = pl.pallas_call(
        pack_kernel,
        out_shape=jax.ShapeDtypeStruct((channels // 8, 16, tokens), BF16),
        compiler_params=vmem_limit(8),
    )(signal, kernel_taps)
    packed, table = lax.optimization_barrier((packed, jnp.asarray(table)))
    spread = lax.all_to_all(packed, "seq", split_axis=0, concat_axis=0, tiled=True)
    convolved = pl.pallas_call(
        functools.partial(conv_kernel, places),
        out_shape=jax.ShapeDtypeStruct((seq_count, 16, 128), BF16),
        scratch_shapes=[
            pltpu.VMEM((tokens // 128 * seq_count * 16, 128), F32),
            pltpu.VMEM((16 * held, 6 * tokens), BF16),
            pltpu.VMEM((16 * held, 2 * tokens), F32),
            pltpu.VMEM((seq_count * 16, 128), F32),
            pltpu.VMEM((6 * tokens, 2 * tokens), BF16),
            pltpu.VMEM((turn_rows, tokens), F32),
        ],
        compiler_params=vmem_limit(24),
    )(spread, table)
    returned = lax.all_to_all(convolved, "seq", split_axis=0, concat_axis=0, tiled=True)
    gated = pl.pallas_call(
        gate_kernel, out_shape=jax.ShapeDtypeStruct((tokens, channels), BF16), compiler_params=vmem_limit(8)
    )(returned, signal, gating, skip_gain.reshape(1, channels))
    up_pairs = [(t, (t + 1) % ring) for t in range(ring)]
    down_pairs = [(t, (t - 1) % ring) for t in range(ring)]
    pieces, offsets = [gated], [0]
    up = down = gated
    for n in range(1, ring // 2):
        up = lax.ppermute(up, "tensor", up_pairs)
        down = lax.ppermute(down, "tensor", down_pairs)
        pieces += [up, down]
        offsets += [-n, n]
    up = lax.ppermute(up[: tokens // 2], "tensor", up_pairs)
    down = lax.ppermute(down[tokens // 2 :], "tensor", down_pairs)
    offsets.append(ring // 2)
    index = (lax.axis_index("tensor") + jnp.asarray(offsets, jnp.int32)) % ring
    total, last_weight = pl.pallas_call(
        project_kernel,
        in_specs=[pl.BlockSpec(memory_space=pltpu.SMEM)] + [vmem] * len(pieces) + [pl.BlockSpec(memory_space=pl.ANY)],
        out_specs=[vmem] * 2,
        out_shape=[
            jax.ShapeDtypeStruct((tokens, channels), F32),
            jax.ShapeDtypeStruct((channels, channels), BF16),
        ],
        scratch_shapes=[
            pltpu.VMEM((len(pieces), channels, channels), BF16),
            pltpu.SemaphoreType.DMA((ring,)),
        ],
        compiler_params=vmem_limit(48),
    )(index, *pieces, full_weight)
    return pl.pallas_call(
        finish_kernel, out_shape=jax.ShapeDtypeStruct((tokens, channels), BF16), compiler_params=vmem_limit(8)
    )(total, up, down, last_weight)


def solution(mesh):
    placed = (
        P("seq", "tensor"),
        P("seq", "tensor"),
        P("seq", "tensor"),
        P("tensor"),
        P("seq", "tensor"),
    )
    return jax.shard_map(
        body, mesh=mesh, in_specs=placed, out_specs=P("seq", "tensor"), check_vma=False
    )
```

```python
import functools
import math

import jax
import jax.numpy as jnp
import ml_dtypes
import numpy as np
from jax import lax
from jax.experimental import pallas as pl
from jax.experimental.pallas import tpu as pltpu
from jax.sharding import PartitionSpec as P

F32 = jnp.float32
BF16 = jnp.bfloat16
MIB = 1024 * 1024


def split_np(table):
    high = table.astype(ml_dtypes.bfloat16)
    low = (table - high.astype(np.float64)).astype(ml_dtypes.bfloat16)
    return high, low


def phases(left, right, modulus):
    return (left[:, None] * right[None, :] % modulus) * (2.0 * math.pi / modulus)


def dft_tables(blocks, inner):
    outer = 2 * blocks
    length = outer * inner
    freqs = blocks + 1
    held = -(-freqs // 8) * 8
    f = np.arange(freqs)
    b = np.arange(blocks)
    i = np.arange(inner)
    first = np.zeros((2 * held, blocks))
    angle = phases(f, b, outer)
    first[:freqs] = np.cos(angle)
    first[held : held + freqs] = -np.sin(angle)
    turn = np.zeros((2 * held, inner))
    turn[:freqs] = np.cos(phases(f, i, length))
    turn[held : held + freqs] = np.sin(phases(f, i, length))
    angle = phases(i, i, inner)
    mid = np.concatenate([np.cos(angle), np.sin(angle)], axis=1)
    weight = np.where((f == 0) | (f == blocks), 1.0, 2.0) / length
    last = np.zeros((blocks, 2 * held))
    angle = phases(b, f, outer)
    last[:, :freqs] = np.cos(angle) * weight
    last[:, held : held + freqs] = -np.sin(angle) * weight
    last_high, last_low = split_np(last)
    parts = [
        np.concatenate(split_np(mid), axis=0),
        np.concatenate(split_np(turn), axis=1),
        np.concatenate(split_np(first), axis=1),
        np.concatenate([last_high, last_high, last_low], axis=1),
    ]
    width = 2 * inner
    table = np.concatenate([np.pad(part, ((0, 0), (0, width - part.shape[1]))) for part in parts], axis=0)
    ends = np.cumsum([part.shape[0] for part in parts])
    return table, [(int(end) - part.shape[0], int(end), part.shape[1]) for end, part in zip(ends, parts)]


def split(values):
    high = values.astype(BF16)
    low = (values - high.astype(F32)).astype(BF16)
    return high, low


def pack_kernel(signal_ref, taps_ref, out_ref):
    tokens, channels = signal_ref.shape
    sig = signal_ref[...].astype(F32).T.reshape(channels // 8, 8, tokens)
    ker = taps_ref[...].T.reshape(channels // 8, 8, tokens)
    out_ref[...] = jnp.concatenate([sig, ker], axis=1).astype(BF16)


def spread_mid(short, mid):
    inner = short.shape[1] // 2
    for n, rows in enumerate((0, inner)):
        cos, sin = short[rows : rows + inner, :inner], short[rows : rows + inner, inner:]
        mid[2 * n * inner : (2 * n + 1) * inner, :inner] = cos
        mid[2 * n * inner : (2 * n + 1) * inner, inner:] = -sin
        mid[(2 * n + 1) * inner : (2 * n + 2) * inner, :inner] = sin
        mid[(2 * n + 1) * inner : (2 * n + 2) * inner, inner:] = cos


def conv_kernel(places, x_ref, table_ref, out_ref, flat, cat, spec, back, mid, turn):
    parts = [table_ref.at[pl.ds(start, end - start), pl.ds(0, width)] for start, end, width in places]
    short_ref, turn_ref, first_ref, last_ref = parts
    held = turn.shape[0] // 2
    spread_mid(short_ref, mid)
    turn[...] = turn_ref[:, : turn.shape[1]].astype(F32) + turn_ref[:, turn.shape[1] :].astype(F32)
    cos_ref, sin_ref = turn.at[pl.ds(0, held)], turn.at[pl.ds(held, held)]
    blocks, rows, inner = x_ref.shape
    chans = rows // 2
    lanes = flat.shape[1]
    halves = inner // lanes
    span = blocks * rows
    for h in range(halves):
        flat[h * span : (h + 1) * span, :] = (
            x_ref[:, :, h * lanes : (h + 1) * lanes].astype(F32).reshape(span, lanes)
        )
    for c in range(chans):
        parts = []
        for row in (c, chans + c):
            x = jnp.concatenate(
                [flat[pl.ds(h * span + row, blocks, stride=rows), :] for h in range(halves)], axis=1
            ).astype(BF16)
            a = jnp.dot(first_ref[...], jnp.concatenate([x, x], axis=0), preferred_element_type=F32)
            real, imag = a[:held], a[held:]
            parts.append(
                jnp.concatenate(
                    [real * cos_ref[...] + imag * sin_ref[...], imag * cos_ref[...] - real * sin_ref[...]], axis=1
                )
            )
        both = jnp.concatenate(parts, axis=0).astype(BF16)
        here = pl.ds(c * 2 * held, 2 * held)
        cat[here, : 2 * inner] = both
        cat[here, 2 * inner :] = both
    spec[...] = jnp.dot(cat[...], mid[...], preferred_element_type=F32)
    for c in range(0, chans, 2):
        parts = []
        for one in (c, c + 1):
            s = spec[pl.ds(one * 2 * held, held), :]
            k = spec[pl.ds(one * 2 * held + held, held), :]
            sr, si, kr, ki = s[:, :inner], s[:, inner:], k[:, :inner], k[:, inner:]
            parts.append(jnp.concatenate([sr * kr - si * ki, -(sr * ki + si * kr)], axis=1))
        both = jnp.concatenate(parts, axis=0).astype(BF16)
        here = pl.ds(c * held, 2 * held)
        cat[here, : 2 * inner] = both
        cat[here, 2 * inner :] = both
    half = chans * held
    spec[:half, :] = jnp.dot(cat[:half, :], mid[...], preferred_element_type=F32)
    for c in range(chans):
        q = spec[pl.ds(c * held, held), :]
        qr, qi = q[:, :inner], -q[:, inner:]
        v = jnp.concatenate(
            [qr * cos_ref[...] - qi * sin_ref[...], qr * sin_ref[...] + qi * cos_ref[...]], axis=0
        )
        high, low = split(v)
        y = jnp.dot(last_ref[...], jnp.concatenate([high, low, high], axis=0), preferred_element_type=F32)
        for h in range(inner // lanes):
            back[pl.ds(h * chans + c, blocks, stride=rows), :] = y[:, h * lanes : (h + 1) * lanes]
    out_ref[...] = back[...].reshape(blocks, rows, lanes).astype(BF16)


def gate_kernel(back_ref, signal_ref, gating_ref, skip_ref, out_ref):
    groups, rows, lanes = back_ref.shape
    chans = 8
    tokens, channels = signal_ref.shape
    y = back_ref[...].astype(F32)
    for h in range(tokens // lanes):
        conv = y[:, h * chans : (h + 1) * chans, :].reshape(channels, lanes).T
        here = pl.ds(h * lanes, lanes)
        mixed = conv + skip_ref[...] * signal_ref[here, :].astype(F32)
        out_ref[here, :] = (gating_ref[here, :].astype(F32) * mixed).astype(BF16)


def project_kernel(index_ref, *refs):
    *pieces, w_ref, total_ref, last_ref, held, arrived = refs
    depth = held.shape[1]
    copies = []
    for n in range(len(pieces) + 1):
        rows = pl.ds(pl.multiple_of(index_ref[n] * depth, depth), depth)
        target = held.at[n] if n < len(pieces) else last_ref
        copies.append(pltpu.make_async_copy(w_ref.at[rows, :], target, arrived.at[n]))
        copies[n].start()
    total = None
    for n, piece in enumerate(pieces):
        copies[n].wait()
        product = jnp.dot(piece[...], held[n], preferred_element_type=F32)
        total = product if total is None else total + product
    total_ref[...] = total
    copies[-1].wait()


def finish_kernel(total_ref, up_ref, down_ref, w_ref, out_ref):
    piece = jnp.concatenate([up_ref[...], down_ref[...]], axis=0)
    product = jnp.dot(piece, w_ref[...], preferred_element_type=F32)
    out_ref[...] = (total_ref[...] + product).astype(BF16)


def vmem_limit(mebibytes):
    return pltpu.CompilerParams(vmem_limit_bytes=mebibytes * MIB)


def body(signal, kernel_taps, gating, skip_gain, out_weight):
    seq_count = lax.axis_size("seq")
    ring = lax.axis_size("tensor")
    tokens, channels = signal.shape
    full_weight = lax.all_gather(out_weight, "seq", axis=0, tiled=True)
    table, places = dft_tables(seq_count, tokens)
    turn_rows = places[1][1] - places[1][0]
    held = turn_rows // 2
    vmem = pl.BlockSpec(memory_space=pltpu.VMEM)
    packed = pl.pallas_call(
        pack_kernel,
        out_shape=jax.ShapeDtypeStruct((channels // 8, 16, tokens), BF16),
        compiler_params=vmem_limit(8),
    )(signal, kernel_taps)
    packed, table = lax.optimization_barrier((packed, jnp.asarray(table)))
    spread = lax.all_to_all(packed, "seq", split_axis=0, concat_axis=0, tiled=True)
    convolved = pl.pallas_call(
        functools.partial(conv_kernel, places),
        out_shape=jax.ShapeDtypeStruct((seq_count, 16, 128), BF16),
        scratch_shapes=[
            pltpu.VMEM((tokens // 128 * seq_count * 16, 128), F32),
            pltpu.VMEM((16 * held, 4 * tokens), BF16),
            pltpu.VMEM((16 * held, 2 * tokens), F32),
            pltpu.VMEM((seq_count * 16, 128), F32),
            pltpu.VMEM((4 * tokens, 2 * tokens), BF16),
            pltpu.VMEM((turn_rows, tokens), F32),
        ],
        compiler_params=vmem_limit(24),
    )(spread, table)
    returned = lax.all_to_all(convolved, "seq", split_axis=0, concat_axis=0, tiled=True)
    gated = pl.pallas_call(
        gate_kernel, out_shape=jax.ShapeDtypeStruct((tokens, channels), BF16), compiler_params=vmem_limit(8)
    )(returned, signal, gating, skip_gain.reshape(1, channels))
    up_pairs = [(t, (t + 1) % ring) for t in range(ring)]
    down_pairs = [(t, (t - 1) % ring) for t in range(ring)]
    pieces, offsets = [gated], [0]
    up = down = gated
    for n in range(1, ring // 2):
        up = lax.ppermute(up, "tensor", up_pairs)
        down = lax.ppermute(down, "tensor", down_pairs)
        pieces += [up, down]
        offsets += [-n, n]
    up = lax.ppermute(up[: tokens // 2], "tensor", up_pairs)
    down = lax.ppermute(down[tokens // 2 :], "tensor", down_pairs)
    offsets.append(ring // 2)
    index = (lax.axis_index("tensor") + jnp.asarray(offsets, jnp.int32)) % ring
    total, last_weight = pl.pallas_call(
        project_kernel,
        in_specs=[pl.BlockSpec(memory_space=pltpu.SMEM)] + [vmem] * len(pieces) + [pl.BlockSpec(memory_space=pl.ANY)],
        out_specs=[vmem] * 2,
        out_shape=[
            jax.ShapeDtypeStruct((tokens, channels), F32),
            jax.ShapeDtypeStruct((channels, channels), BF16),
        ],
        scratch_shapes=[
            pltpu.VMEM((len(pieces), channels, channels), BF16),
            pltpu.SemaphoreType.DMA((ring,)),
        ],
        compiler_params=vmem_limit(48),
    )(index, *pieces, full_weight)
    return pl.pallas_call(
        finish_kernel, out_shape=jax.ShapeDtypeStruct((tokens, channels), BF16), compiler_params=vmem_limit(8)
    )(total, up, down, last_weight)


def solution(mesh):
    placed = (
        P("seq", "tensor"),
        P("seq", "tensor"),
        P("seq", "tensor"),
        P("tensor"),
        P("seq", "tensor"),
    )
    return jax.shard_map(
        body, mesh=mesh, in_specs=placed, out_specs=P("seq", "tensor"), check_vma=False
    )
```

```python
import functools
import math

import jax
import jax.numpy as jnp
import ml_dtypes
import numpy as np
from jax import lax
from jax.experimental import pallas as pl
from jax.experimental.pallas import tpu as pltpu
from jax.sharding import PartitionSpec as P

F32 = jnp.float32
BF16 = jnp.bfloat16
MIB = 1024 * 1024


def split_np(table):
    high = table.astype(ml_dtypes.bfloat16)
    low = (table - high.astype(np.float64)).astype(ml_dtypes.bfloat16)
    return high, low


def phases(left, right, modulus):
    return (left[:, None] * right[None, :] % modulus) * (2.0 * math.pi / modulus)


def dft_tables(blocks, inner):
    outer = 2 * blocks
    length = outer * inner
    freqs = blocks + 1
    held = -(-freqs // 8) * 8
    f = np.arange(freqs)
    b = np.arange(blocks)
    i = np.arange(inner)
    first = np.zeros((2 * held, blocks))
    angle = phases(f, b, outer)
    first[:freqs] = np.cos(angle)
    first[held : held + freqs] = -np.sin(angle)
    turn = np.zeros((2 * held, inner))
    turn[:freqs] = np.cos(phases(f, i, length))
    turn[held : held + freqs] = np.sin(phases(f, i, length))
    angle = phases(i, i, inner)
    mid = np.concatenate([np.cos(angle), np.sin(angle)], axis=1)
    weight = np.where((f == 0) | (f == blocks), 1.0, 2.0) / length
    last = np.zeros((blocks, 2 * held))
    angle = phases(b, f, outer)
    last[:, :freqs] = np.cos(angle) * weight
    last[:, held : held + freqs] = -np.sin(angle) * weight
    last_high, last_low = split_np(last)
    parts = [
        np.concatenate(split_np(mid), axis=0),
        np.concatenate(split_np(turn), axis=1),
        np.concatenate(split_np(first), axis=1),
        np.concatenate([last_high, last_high, last_low], axis=1),
    ]
    width = 2 * inner
    table = np.concatenate([np.pad(part, ((0, 0), (0, width - part.shape[1]))) for part in parts], axis=0)
    ends = np.cumsum([part.shape[0] for part in parts])
    return table, [(int(end) - part.shape[0], int(end), part.shape[1]) for end, part in zip(ends, parts)]


def split(values):
    high = values.astype(BF16)
    low = (values - high.astype(F32)).astype(BF16)
    return high, low


def pack_kernel(signal_ref, taps_ref, out_ref):
    tokens, channels = signal_ref.shape
    sig = signal_ref[...].astype(F32).T.reshape(channels // 8, 8, tokens)
    ker = taps_ref[...].T.reshape(channels // 8, 8, tokens)
    out_ref[...] = jnp.concatenate([sig, ker], axis=1).astype(BF16)


def spread_mid(short, mid):
    inner = short.shape[1] // 2
    for n, rows in enumerate((0, inner)):
        cos, sin = short[rows : rows + inner, :inner], short[rows : rows + inner, inner:]
        mid[2 * n * inner : (2 * n + 1) * inner, :inner] = cos
        mid[2 * n * inner : (2 * n + 1) * inner, inner:] = -sin
        mid[(2 * n + 1) * inner : (2 * n + 2) * inner, :inner] = sin
        mid[(2 * n + 1) * inner : (2 * n + 2) * inner, inner:] = cos


def conv_kernel(places, x_ref, table_ref, out_ref, flat, cat, spec, back, mid, turn):
    parts = [table_ref.at[pl.ds(start, end - start), pl.ds(0, width)] for start, end, width in places]
    short_ref, turn_ref, first_ref, last_ref = parts
    held = turn.shape[0] // 2
    spread_mid(short_ref, mid)
    turn[...] = turn_ref[:, : turn.shape[1]].astype(F32) + turn_ref[:, turn.shape[1] :].astype(F32)
    cos_ref, sin_ref = turn.at[pl.ds(0, held)], turn.at[pl.ds(held, held)]
    blocks, rows, inner = x_ref.shape
    chans = rows // 2
    lanes = flat.shape[1]
    halves = inner // lanes
    span = blocks * rows
    for h in range(halves):
        flat[h * span : (h + 1) * span, :] = (
            x_ref[:, :, h * lanes : (h + 1) * lanes].astype(F32).reshape(span, lanes)
        )
    for c in range(chans):
        parts = []
        for row in (c, chans + c):
            x = jnp.concatenate(
                [flat[pl.ds(h * span + row, blocks, stride=rows), :] for h in range(halves)], axis=1
            ).astype(BF16)
            a = jnp.dot(first_ref[...], jnp.concatenate([x, x], axis=0), preferred_element_type=F32)
            real, imag = a[:held], a[held:]
            parts.append(
                jnp.concatenate(
                    [real * cos_ref[...] + imag * sin_ref[...], imag * cos_ref[...] - real * sin_ref[...]], axis=1
                )
            )
        both = jnp.concatenate(parts, axis=0).astype(BF16)
        here = pl.ds(c * 2 * held, 2 * held)
        cat[here, : 2 * inner] = both
        cat[here, 2 * inner :] = both
    spec[...] = jnp.dot(cat[...], mid[...], preferred_element_type=F32)
    for c in range(0, chans, 2):
        parts = []
        for one in (c, c + 1):
            s = spec[pl.ds(one * 2 * held, held), :]
            k = spec[pl.ds(one * 2 * held + held, held), :]
            sr, si, kr, ki = s[:, :inner], s[:, inner:], k[:, :inner], k[:, inner:]
            parts.append(jnp.concatenate([sr * kr - si * ki, -(sr * ki + si * kr)], axis=1))
        both = jnp.concatenate(parts, axis=0).astype(BF16)
        here = pl.ds(c * held, 2 * held)
        cat[here, : 2 * inner] = both
        cat[here, 2 * inner :] = both
    half = chans * held
    spec[:half, :] = jnp.dot(cat[:half, :], mid[...], preferred_element_type=F32)
    for c in range(chans):
        q = spec[pl.ds(c * held, held), :]
        qr, qi = q[:, :inner], -q[:, inner:]
        v = jnp.concatenate(
            [qr * cos_ref[...] - qi * sin_ref[...], qr * sin_ref[...] + qi * cos_ref[...]], axis=0
        )
        high, low = split(v)
        y = jnp.dot(last_ref[...], jnp.concatenate([high, low, high], axis=0), preferred_element_type=F32)
        for h in range(inner // lanes):
            back[pl.ds(h * chans + c, blocks, stride=rows), :] = y[:, h * lanes : (h + 1) * lanes]
    out_ref[...] = back[...].reshape(blocks, rows, lanes).astype(BF16)


def gate_kernel(back_ref, signal_ref, gating_ref, skip_ref, out_ref):
    groups, rows, lanes = back_ref.shape
    chans = 8
    tokens, channels = signal_ref.shape
    y = back_ref[...].astype(F32)
    for h in range(tokens // lanes):
        conv = y[:, h * chans : (h + 1) * chans, :].reshape(channels, lanes).T
        here = pl.ds(h * lanes, lanes)
        mixed = conv + skip_ref[...] * signal_ref[here, :].astype(F32)
        out_ref[here, :] = (gating_ref[here, :].astype(F32) * mixed).astype(BF16)


def project_kernel(index_ref, *refs):
    *pieces, w_ref, total_ref, last_ref, held, arrived = refs
    depth = held.shape[1]
    copies = []
    for n in range(len(pieces) + 1):
        rows = pl.ds(pl.multiple_of(index_ref[n] * depth, depth), depth)
        target = held.at[n] if n < len(pieces) else last_ref
        copies.append(pltpu.make_async_copy(w_ref.at[rows, :], target, arrived.at[n]))
        copies[n].start()
    total = None
    for n, piece in enumerate(pieces):
        copies[n].wait()
        product = jnp.dot(piece[...], held[n], preferred_element_type=F32)
        total = product if total is None else total + product
    total_ref[...] = total
    copies[-1].wait()


def finish_kernel(total_ref, up_ref, down_ref, w_ref, out_ref):
    piece = jnp.concatenate([up_ref[...], down_ref[...]], axis=0)
    product = jnp.dot(piece, w_ref[...], preferred_element_type=F32)
    out_ref[...] = (total_ref[...] + product).astype(BF16)


def vmem_limit(mebibytes):
    return pltpu.CompilerParams(vmem_limit_bytes=mebibytes * MIB)


def body(signal, kernel_taps, gating, skip_gain, out_weight):
    seq_count = lax.axis_size("seq")
    ring = lax.axis_size("tensor")
    tokens, channels = signal.shape
    full_weight = lax.all_gather(out_weight, "seq", axis=0, tiled=True)
    table, places = dft_tables(seq_count, tokens)
    turn_rows = places[1][1] - places[1][0]
    held = turn_rows // 2
    vmem = pl.BlockSpec(memory_space=pltpu.VMEM)
    packed = pl.pallas_call(
        pack_kernel,
        out_shape=jax.ShapeDtypeStruct((channels // 8, 16, tokens), BF16),
        compiler_params=vmem_limit(8),
    )(signal, kernel_taps)
    packed, table = lax.optimization_barrier((packed, jnp.asarray(table)))
    spread = lax.all_to_all(packed, "seq", split_axis=0, concat_axis=0, tiled=True)
    convolved = pl.pallas_call(
        functools.partial(conv_kernel, places),
        out_shape=jax.ShapeDtypeStruct((seq_count, 16, 128), BF16),
        scratch_shapes=[
            pltpu.VMEM((tokens // 128 * seq_count * 16, 128), F32),
            pltpu.VMEM((16 * held, 4 * tokens), BF16),
            pltpu.VMEM((16 * held, 2 * tokens), F32),
            pltpu.VMEM((seq_count * 16, 128), F32),
            pltpu.VMEM((4 * tokens, 2 * tokens), BF16),
            pltpu.VMEM((turn_rows, tokens), F32),
        ],
        compiler_params=vmem_limit(24),
    )(spread, table)
    returned = lax.all_to_all(convolved, "seq", split_axis=0, concat_axis=0, tiled=True)
    gated = pl.pallas_call(
        gate_kernel, out_shape=jax.ShapeDtypeStruct((tokens, channels), BF16), compiler_params=vmem_limit(8)
    )(returned, signal, gating, skip_gain.reshape(1, channels))
    up_pairs = [(t, (t + 1) % ring) for t in range(ring)]
    down_pairs = [(t, (t - 1) % ring) for t in range(ring)]
    up_two = [(t, (t + 2) % ring) for t in range(ring)]
    down_two = [(t, (t - 2) % ring) for t in range(ring)]
    pieces, offsets = [gated], [0]
    up = down = gated
    for n in range(1, ring // 2 - 1):
        up = lax.ppermute(up, "tensor", up_pairs)
        down = lax.ppermute(down, "tensor", down_pairs)
        pieces += [up, down]
        offsets += [-n, n]
    up_next = lax.ppermute(up, "tensor", up_pairs)
    down_next = lax.ppermute(down, "tensor", down_pairs)
    up_far = lax.ppermute(up[: tokens // 2], "tensor", up_two)
    down_far = lax.ppermute(down[tokens // 2 :], "tensor", down_two)
    pieces += [up_next, down_next]
    offsets += [1 - ring // 2, ring // 2 - 1]
    up, down = up_far, down_far
    offsets.append(ring // 2)
    index = (lax.axis_index("tensor") + jnp.asarray(offsets, jnp.int32)) % ring
    total, last_weight = pl.pallas_call(
        project_kernel,
        in_specs=[pl.BlockSpec(memory_space=pltpu.SMEM)] + [vmem] * len(pieces) + [pl.BlockSpec(memory_space=pl.ANY)],
        out_specs=[vmem] * 2,
        out_shape=[
            jax.ShapeDtypeStruct((tokens, channels), F32),
            jax.ShapeDtypeStruct((channels, channels), BF16),
        ],
        scratch_shapes=[
            pltpu.VMEM((len(pieces), channels, channels), BF16),
            pltpu.SemaphoreType.DMA((ring,)),
        ],
        compiler_params=vmem_limit(48),
    )(index, *pieces, full_weight)
    return pl.pallas_call(
        finish_kernel, out_shape=jax.ShapeDtypeStruct((tokens, channels), BF16), compiler_params=vmem_limit(8)
    )(total, up, down, last_weight)


def solution(mesh):
    placed = (
        P("seq", "tensor"),
        P("seq", "tensor"),
        P("seq", "tensor"),
        P("tensor"),
        P("seq", "tensor"),
    )
    return jax.shard_map(
        body, mesh=mesh, in_specs=placed, out_specs=P("seq", "tensor"), check_vma=False
    )
```

```python
import functools
import math

import jax
import jax.numpy as jnp
import ml_dtypes
import numpy as np
from jax import lax
from jax.experimental import pallas as pl
from jax.experimental.pallas import tpu as pltpu
from jax.sharding import PartitionSpec as P

F32 = jnp.float32
BF16 = jnp.bfloat16
MIB = 1024 * 1024


def split_np(table):
    high = table.astype(ml_dtypes.bfloat16)
    low = (table - high.astype(np.float64)).astype(ml_dtypes.bfloat16)
    return high, low


def phases(left, right, modulus):
    return (left[:, None] * right[None, :] % modulus) * (2.0 * math.pi / modulus)


def dft_tables(blocks, inner):
    outer = 2 * blocks
    length = outer * inner
    freqs = blocks + 1
    held = -(-freqs // 8) * 8
    f = np.arange(freqs)
    b = np.arange(blocks)
    i = np.arange(inner)
    first = np.zeros((2 * held, blocks))
    angle = phases(f, b, outer)
    first[:freqs] = np.cos(angle)
    first[held : held + freqs] = -np.sin(angle)
    turn = np.zeros((2 * held, inner))
    turn[:freqs] = np.cos(phases(f, i, length))
    turn[held : held + freqs] = np.sin(phases(f, i, length))
    angle = phases(i, i, inner)
    mid = np.concatenate([np.cos(angle), np.sin(angle)], axis=1)
    weight = np.where((f == 0) | (f == blocks), 1.0, 2.0) / length
    last = np.zeros((blocks, 2 * held))
    angle = phases(b, f, outer)
    last[:, :freqs] = np.cos(angle) * weight
    last[:, held : held + freqs] = -np.sin(angle) * weight
    last_high, last_low = split_np(last)
    parts = [
        np.concatenate(split_np(mid), axis=0),
        np.concatenate(split_np(turn), axis=1),
        np.concatenate(split_np(first), axis=1),
        np.concatenate([last_high, last_high, last_low], axis=1),
    ]
    width = 2 * inner
    table = np.concatenate([np.pad(part, ((0, 0), (0, width - part.shape[1]))) for part in parts], axis=0)
    ends = np.cumsum([part.shape[0] for part in parts])
    return table, [(int(end) - part.shape[0], int(end), part.shape[1]) for end, part in zip(ends, parts)]


def split(values):
    high = values.astype(BF16)
    low = (values - high.astype(F32)).astype(BF16)
    return high, low


def pack_kernel(signal_ref, taps_ref, out_ref):
    tokens, channels = signal_ref.shape
    sig = signal_ref[...].astype(F32).T.reshape(channels // 8, 8, tokens)
    ker = taps_ref[...].T.reshape(channels // 8, 8, tokens)
    out_ref[...] = jnp.concatenate([sig, ker], axis=1).astype(BF16)


def spread_mid(short, mid):
    inner = short.shape[1] // 2
    for n, rows in enumerate((0, 0, inner)):
        cos, sin = short[rows : rows + inner, :inner], short[rows : rows + inner, inner:]
        mid[2 * n * inner : (2 * n + 1) * inner, :inner] = cos
        mid[2 * n * inner : (2 * n + 1) * inner, inner:] = -sin
        mid[(2 * n + 1) * inner : (2 * n + 2) * inner, :inner] = sin
        mid[(2 * n + 1) * inner : (2 * n + 2) * inner, inner:] = cos


def conv_kernel(places, x_ref, table_ref, out_ref, flat, cat, spec, back, mid, turn):
    parts = [table_ref.at[pl.ds(start, end - start), pl.ds(0, width)] for start, end, width in places]
    short_ref, turn_ref, first_ref, last_ref = parts
    held = turn.shape[0] // 2
    spread_mid(short_ref, mid)
    turn[...] = turn_ref[:, : turn.shape[1]].astype(F32) + turn_ref[:, turn.shape[1] :].astype(F32)
    cos_ref, sin_ref = turn.at[pl.ds(0, held)], turn.at[pl.ds(held, held)]
    blocks, rows, inner = x_ref.shape
    chans = rows // 2
    lanes = flat.shape[1]
    halves = inner // lanes
    span = blocks * rows
    for h in range(halves):
        flat[h * span : (h + 1) * span, :] = (
            x_ref[:, :, h * lanes : (h + 1) * lanes].astype(F32).reshape(span, lanes)
        )
    for c in range(chans):
        parts = []
        for row in (c, chans + c):
            x = jnp.concatenate(
                [flat[pl.ds(h * span + row, blocks, stride=rows), :] for h in range(halves)], axis=1
            ).astype(BF16)
            a = jnp.dot(first_ref[...], jnp.concatenate([x, x], axis=0), preferred_element_type=F32)
            real, imag = a[:held], a[held:]
            parts.append(
                jnp.concatenate(
                    [real * cos_ref[...] + imag * sin_ref[...], imag * cos_ref[...] - real * sin_ref[...]], axis=1
                )
            )
        high, low = split(jnp.concatenate(parts, axis=0))
        here = pl.ds(c * 2 * held, 2 * held)
        cat[here, : 2 * inner] = high
        cat[here, 2 * inner : 4 * inner] = low
        cat[here, 4 * inner :] = high
    spec[...] = jnp.dot(cat[...], mid[...], preferred_element_type=F32)
    for c in range(0, chans, 2):
        parts = []
        for one in (c, c + 1):
            s = spec[pl.ds(one * 2 * held, held), :]
            k = spec[pl.ds(one * 2 * held + held, held), :]
            sr, si, kr, ki = s[:, :inner], s[:, inner:], k[:, :inner], k[:, inner:]
            parts.append(jnp.concatenate([sr * kr - si * ki, -(sr * ki + si * kr)], axis=1))
        high, low = split(jnp.concatenate(parts, axis=0))
        here = pl.ds(c * held, 2 * held)
        cat[here, : 2 * inner] = high
        cat[here, 2 * inner : 4 * inner] = low
        cat[here, 4 * inner :] = high
    half = chans * held
    spec[:half, :] = jnp.dot(cat[:half, :], mid[...], preferred_element_type=F32)
    for c in range(chans):
        q = spec[pl.ds(c * held, held), :]
        qr, qi = q[:, :inner], -q[:, inner:]
        v = jnp.concatenate(
            [qr * cos_ref[...] - qi * sin_ref[...], qr * sin_ref[...] + qi * cos_ref[...]], axis=0
        )
        high, low = split(v)
        y = jnp.dot(last_ref[...], jnp.concatenate([high, low, high], axis=0), preferred_element_type=F32)
        for h in range(inner // lanes):
            back[pl.ds(h * chans + c, blocks, stride=rows), :] = y[:, h * lanes : (h + 1) * lanes]
    out_ref[...] = back[...].reshape(blocks, rows, lanes).astype(BF16)


def gate_kernel(back_ref, signal_ref, gating_ref, skip_ref, out_ref):
    groups, rows, lanes = back_ref.shape
    chans = 8
    tokens, channels = signal_ref.shape
    y = back_ref[...].astype(F32)
    for h in range(tokens // lanes):
        conv = y[:, h * chans : (h + 1) * chans, :].reshape(channels, lanes).T
        here = pl.ds(h * lanes, lanes)
        mixed = conv + skip_ref[...] * signal_ref[here, :].astype(F32)
        out_ref[here, :] = (gating_ref[here, :].astype(F32) * mixed).astype(BF16)


def project_kernel(index_ref, *refs):
    *pieces, w_ref, total_ref, last_ref, held, arrived = refs
    depth = held.shape[1]
    copies = []
    for n in range(len(pieces) + 1):
        rows = pl.ds(pl.multiple_of(index_ref[n] * depth, depth), depth)
        target = held.at[n] if n < len(pieces) else last_ref
        copies.append(pltpu.make_async_copy(w_ref.at[rows, :], target, arrived.at[n]))
        copies[n].start()
    total = None
    for n, piece in enumerate(pieces):
        copies[n].wait()
        product = jnp.dot(piece[...], held[n], preferred_element_type=F32)
        total = product if total is None else total + product
    total_ref[...] = total
    copies[-1].wait()


def finish_kernel(total_ref, up_ref, down_ref, w_ref, out_ref):
    piece = jnp.concatenate([up_ref[...], down_ref[...]], axis=0)
    product = jnp.dot(piece, w_ref[...], preferred_element_type=F32)
    out_ref[...] = (total_ref[...] + product).astype(BF16)


def vmem_limit(mebibytes):
    return pltpu.CompilerParams(vmem_limit_bytes=mebibytes * MIB)


def body(signal, kernel_taps, gating, skip_gain, out_weight):
    seq_count = lax.axis_size("seq")
    ring = lax.axis_size("tensor")
    tokens, channels = signal.shape
    full_weight = lax.all_gather(out_weight, "seq", axis=0, tiled=True)
    table, places = dft_tables(seq_count, tokens)
    turn_rows = places[1][1] - places[1][0]
    held = turn_rows // 2
    vmem = pl.BlockSpec(memory_space=pltpu.VMEM)
    packed = pl.pallas_call(
        pack_kernel,
        out_shape=jax.ShapeDtypeStruct((channels // 8, 16, tokens), BF16),
        compiler_params=vmem_limit(8),
    )(signal, kernel_taps)
    packed, table = lax.optimization_barrier((packed, jnp.asarray(table)))
    spread = lax.all_to_all(packed, "seq", split_axis=0, concat_axis=0, tiled=True)
    convolved = pl.pallas_call(
        functools.partial(conv_kernel, places),
        out_shape=jax.ShapeDtypeStruct((seq_count, 16, 128), BF16),
        scratch_shapes=[
            pltpu.VMEM((tokens // 128 * seq_count * 16, 128), F32),
            pltpu.VMEM((16 * held, 6 * tokens), BF16),
            pltpu.VMEM((16 * held, 2 * tokens), F32),
            pltpu.VMEM((seq_count * 16, 128), F32),
            pltpu.VMEM((6 * tokens, 2 * tokens), BF16),
            pltpu.VMEM((turn_rows, tokens), F32),
        ],
        compiler_params=vmem_limit(24),
    )(spread, table)
    returned = lax.all_to_all(convolved, "seq", split_axis=0, concat_axis=0, tiled=True)
    gated = pl.pallas_call(
        gate_kernel, out_shape=jax.ShapeDtypeStruct((tokens, channels), BF16), compiler_params=vmem_limit(8)
    )(returned, signal, gating, skip_gain.reshape(1, channels))
    up_pairs = [(t, (t + 1) % ring) for t in range(ring)]
    down_pairs = [(t, (t - 1) % ring) for t in range(ring)]
    up_two = [(t, (t + 2) % ring) for t in range(ring)]
    down_two = [(t, (t - 2) % ring) for t in range(ring)]
    pieces, offsets = [gated], [0]
    up = down = gated
    for n in range(1, ring // 2 - 1):
        up = lax.ppermute(up, "tensor", up_pairs)
        down = lax.ppermute(down, "tensor", down_pairs)
        pieces += [up, down]
        offsets += [-n, n]
    up_next = lax.ppermute(up, "tensor", up_pairs)
    down_next = lax.ppermute(down, "tensor", down_pairs)
    up_far = lax.ppermute(up[: tokens // 2], "tensor", up_two)
    down_far = lax.ppermute(down[tokens // 2 :], "tensor", down_two)
    pieces += [up_next, down_next]
    offsets += [1 - ring // 2, ring // 2 - 1]
    up, down = up_far, down_far
    offsets.append(ring // 2)
    index = (lax.axis_index("tensor") + jnp.asarray(offsets, jnp.int32)) % ring
    total, last_weight = pl.pallas_call(
        project_kernel,
        in_specs=[pl.BlockSpec(memory_space=pltpu.SMEM)] + [vmem] * len(pieces) + [pl.BlockSpec(memory_space=pl.ANY)],
        out_specs=[vmem] * 2,
        out_shape=[
            jax.ShapeDtypeStruct((tokens, channels), F32),
            jax.ShapeDtypeStruct((channels, channels), BF16),
        ],
        scratch_shapes=[
            pltpu.VMEM((len(pieces), channels, channels), BF16),
            pltpu.SemaphoreType.DMA((ring,)),
        ],
        compiler_params=vmem_limit(48),
    )(index, *pieces, full_weight)
    return pl.pallas_call(
        finish_kernel, out_shape=jax.ShapeDtypeStruct((tokens, channels), BF16), compiler_params=vmem_limit(8)
    )(total, up, down, last_weight)


def solution(mesh):
    placed = (
        P("seq", "tensor"),
        P("seq", "tensor"),
        P("seq", "tensor"),
        P("tensor"),
        P("seq", "tensor"),
    )
    return jax.shard_map(
        body, mesh=mesh, in_specs=placed, out_specs=P("seq", "tensor"), check_vma=False
    )
```

```python
import functools
import math

import jax
import jax.numpy as jnp
import ml_dtypes
import numpy as np
from jax import lax
from jax.experimental import pallas as pl
from jax.experimental.pallas import tpu as pltpu
from jax.sharding import PartitionSpec as P

F32 = jnp.float32
BF16 = jnp.bfloat16
MIB = 1024 * 1024


def split_np(table):
    high = table.astype(ml_dtypes.bfloat16)
    low = (table - high.astype(np.float64)).astype(ml_dtypes.bfloat16)
    return high, low


def phases(left, right, modulus):
    return (left[:, None] * right[None, :] % modulus) * (2.0 * math.pi / modulus)


def dft_tables(blocks, inner):
    outer = 2 * blocks
    length = outer * inner
    freqs = blocks + 1
    held = -(-freqs // 8) * 8
    f = np.arange(freqs)
    b = np.arange(blocks)
    i = np.arange(inner)
    first = np.zeros((2 * held, blocks))
    angle = phases(f, b, outer)
    first[:freqs] = np.cos(angle)
    first[held : held + freqs] = -np.sin(angle)
    turn = np.zeros((2 * held, inner))
    turn[:freqs] = np.cos(phases(f, i, length))
    turn[held : held + freqs] = np.sin(phases(f, i, length))
    angle = phases(i, i, inner)
    mid = np.concatenate([np.cos(angle), np.sin(angle)], axis=1)
    weight = np.where((f == 0) | (f == blocks), 1.0, 2.0) / length
    last = np.zeros((blocks, 2 * held))
    angle = phases(b, f, outer)
    last[:, :freqs] = np.cos(angle) * weight
    last[:, held : held + freqs] = -np.sin(angle) * weight
    last_high, last_low = split_np(last)
    parts = [
        np.concatenate(split_np(mid), axis=0),
        np.concatenate(split_np(turn), axis=1),
        np.concatenate(split_np(first), axis=1),
        np.concatenate([last_high, last_high, last_low], axis=1),
    ]
    width = 2 * inner
    table = np.concatenate([np.pad(part, ((0, 0), (0, width - part.shape[1]))) for part in parts], axis=0)
    ends = np.cumsum([part.shape[0] for part in parts])
    return table, [(int(end) - part.shape[0], int(end), part.shape[1]) for end, part in zip(ends, parts)]


def split(values):
    high = values.astype(BF16)
    low = (values - high.astype(F32)).astype(BF16)
    return high, low


def pack_kernel(signal_ref, taps_ref, out_ref):
    tokens, channels = signal_ref.shape
    sig = signal_ref[...].astype(F32).T.reshape(channels // 8, 8, tokens)
    ker = taps_ref[...].T.reshape(channels // 8, 8, tokens)
    out_ref[...] = jnp.concatenate([sig, ker], axis=1).astype(BF16)


def spread_mid(short, mid):
    inner = short.shape[1] // 2
    for n, rows in enumerate((0, inner)):
        cos, sin = short[rows : rows + inner, :inner], short[rows : rows + inner, inner:]
        mid[2 * n * inner : (2 * n + 1) * inner, :inner] = cos
        mid[2 * n * inner : (2 * n + 1) * inner, inner:] = -sin
        mid[(2 * n + 1) * inner : (2 * n + 2) * inner, :inner] = sin
        mid[(2 * n + 1) * inner : (2 * n + 2) * inner, inner:] = cos


def three_products(cat, mid, rows):
    depth = mid.shape[0] // 2
    product = jnp.dot(cat[:rows, :depth], mid[:depth, :], preferred_element_type=F32)
    product += jnp.dot(cat[:rows, :depth], mid[depth:, :], preferred_element_type=F32)
    return product + jnp.dot(cat[:rows, depth:], mid[:depth, :], preferred_element_type=F32)


def conv_kernel(places, x_ref, table_ref, out_ref, flat, cat, spec, back, mid, turn):
    parts = [table_ref.at[pl.ds(start, end - start), pl.ds(0, width)] for start, end, width in places]
    short_ref, turn_ref, first_ref, last_ref = parts
    held = turn.shape[0] // 2
    spread_mid(short_ref, mid)
    turn[...] = turn_ref[:, : turn.shape[1]].astype(F32) + turn_ref[:, turn.shape[1] :].astype(F32)
    cos_ref, sin_ref = turn.at[pl.ds(0, held)], turn.at[pl.ds(held, held)]
    blocks, rows, inner = x_ref.shape
    chans = rows // 2
    lanes = flat.shape[1]
    halves = inner // lanes
    span = blocks * rows
    for h in range(halves):
        flat[h * span : (h + 1) * span, :] = (
            x_ref[:, :, h * lanes : (h + 1) * lanes].astype(F32).reshape(span, lanes)
        )
    for c in range(chans):
        parts = []
        for row in (c, chans + c):
            x = jnp.concatenate(
                [flat[pl.ds(h * span + row, blocks, stride=rows), :] for h in range(halves)], axis=1
            ).astype(BF16)
            a = jnp.dot(first_ref[...], jnp.concatenate([x, x], axis=0), preferred_element_type=F32)
            real, imag = a[:held], a[held:]
            parts.append(
                jnp.concatenate(
                    [real * cos_ref[...] + imag * sin_ref[...], imag * cos_ref[...] - real * sin_ref[...]], axis=1
                )
            )
        high, low = split(jnp.concatenate(parts, axis=0))
        here = pl.ds(c * 2 * held, 2 * held)
        cat[here, : 2 * inner] = high
        cat[here, 2 * inner :] = low
    spec[...] = three_products(cat, mid, chans * 2 * held)
    for c in range(0, chans, 2):
        parts = []
        for one in (c, c + 1):
            s = spec[pl.ds(one * 2 * held, held), :]
            k = spec[pl.ds(one * 2 * held + held, held), :]
            sr, si, kr, ki = s[:, :inner], s[:, inner:], k[:, :inner], k[:, inner:]
            parts.append(jnp.concatenate([sr * kr - si * ki, -(sr * ki + si * kr)], axis=1))
        high, low = split(jnp.concatenate(parts, axis=0))
        here = pl.ds(c * held, 2 * held)
        cat[here, : 2 * inner] = high
        cat[here, 2 * inner :] = low
    half = chans * held
    spec[:half, :] = three_products(cat, mid, half)
    for c in range(chans):
        q = spec[pl.ds(c * held, held), :]
        qr, qi = q[:, :inner], -q[:, inner:]
        v = jnp.concatenate(
            [qr * cos_ref[...] - qi * sin_ref[...], qr * sin_ref[...] + qi * cos_ref[...]], axis=0
        )
        high, low = split(v)
        y = jnp.dot(last_ref[...], jnp.concatenate([high, low, high], axis=0), preferred_element_type=F32)
        for h in range(inner // lanes):
            back[pl.ds(h * chans + c, blocks, stride=rows), :] = y[:, h * lanes : (h + 1) * lanes]
    out_ref[...] = back[...].reshape(blocks, rows, lanes).astype(BF16)


def gate_kernel(back_ref, signal_ref, gating_ref, skip_ref, out_ref):
    groups, rows, lanes = back_ref.shape
    chans = 8
    tokens, channels = signal_ref.shape
    y = back_ref[...].astype(F32)
    for h in range(tokens // lanes):
        conv = y[:, h * chans : (h + 1) * chans, :].reshape(channels, lanes).T
        here = pl.ds(h * lanes, lanes)
        mixed = conv + skip_ref[...] * signal_ref[here, :].astype(F32)
        out_ref[here, :] = (gating_ref[here, :].astype(F32) * mixed).astype(BF16)


def project_kernel(index_ref, *refs):
    *pieces, w_ref, total_ref, last_ref, held, arrived = refs
    depth = held.shape[1]
    copies = []
    for n in range(len(pieces) + 1):
        rows = pl.ds(pl.multiple_of(index_ref[n] * depth, depth), depth)
        target = held.at[n] if n < len(pieces) else last_ref
        copies.append(pltpu.make_async_copy(w_ref.at[rows, :], target, arrived.at[n]))
        copies[n].start()
    total = None
    for n, piece in enumerate(pieces):
        copies[n].wait()
        product = jnp.dot(piece[...], held[n], preferred_element_type=F32)
        total = product if total is None else total + product
    total_ref[...] = total
    copies[-1].wait()


def finish_kernel(total_ref, up_ref, down_ref, w_ref, out_ref):
    piece = jnp.concatenate([up_ref[...], down_ref[...]], axis=0)
    product = jnp.dot(piece, w_ref[...], preferred_element_type=F32)
    out_ref[...] = (total_ref[...] + product).astype(BF16)


def vmem_limit(mebibytes):
    return pltpu.CompilerParams(vmem_limit_bytes=mebibytes * MIB)


def body(signal, kernel_taps, gating, skip_gain, out_weight):
    seq_count = lax.axis_size("seq")
    ring = lax.axis_size("tensor")
    tokens, channels = signal.shape
    full_weight = lax.all_gather(out_weight, "seq", axis=0, tiled=True)
    table, places = dft_tables(seq_count, tokens)
    turn_rows = places[1][1] - places[1][0]
    held = turn_rows // 2
    vmem = pl.BlockSpec(memory_space=pltpu.VMEM)
    packed = pl.pallas_call(
        pack_kernel,
        out_shape=jax.ShapeDtypeStruct((channels // 8, 16, tokens), BF16),
        compiler_params=vmem_limit(8),
    )(signal, kernel_taps)
    packed, table = lax.optimization_barrier((packed, jnp.asarray(table)))
    spread = lax.all_to_all(packed, "seq", split_axis=0, concat_axis=0, tiled=True)
    convolved = pl.pallas_call(
        functools.partial(conv_kernel, places),
        out_shape=jax.ShapeDtypeStruct((seq_count, 16, 128), BF16),
        scratch_shapes=[
            pltpu.VMEM((tokens // 128 * seq_count * 16, 128), F32),
            pltpu.VMEM((16 * held, 4 * tokens), BF16),
            pltpu.VMEM((16 * held, 2 * tokens), F32),
            pltpu.VMEM((seq_count * 16, 128), F32),
            pltpu.VMEM((4 * tokens, 2 * tokens), BF16),
            pltpu.VMEM((turn_rows, tokens), F32),
        ],
        compiler_params=vmem_limit(24),
    )(spread, table)
    returned = lax.all_to_all(convolved, "seq", split_axis=0, concat_axis=0, tiled=True)
    gated = pl.pallas_call(
        gate_kernel, out_shape=jax.ShapeDtypeStruct((tokens, channels), BF16), compiler_params=vmem_limit(8)
    )(returned, signal, gating, skip_gain.reshape(1, channels))
    up_pairs = [(t, (t + 1) % ring) for t in range(ring)]
    down_pairs = [(t, (t - 1) % ring) for t in range(ring)]
    pieces, offsets = [gated], [0]
    up = down = gated
    for n in range(1, ring // 2):
        up = lax.ppermute(up, "tensor", up_pairs)
        down = lax.ppermute(down, "tensor", down_pairs)
        pieces += [up, down]
        offsets += [-n, n]
    up = lax.ppermute(up[: tokens // 2], "tensor", up_pairs)
    down = lax.ppermute(down[tokens // 2 :], "tensor", down_pairs)
    offsets.append(ring // 2)
    index = (lax.axis_index("tensor") + jnp.asarray(offsets, jnp.int32)) % ring
    total, last_weight = pl.pallas_call(
        project_kernel,
        in_specs=[pl.BlockSpec(memory_space=pltpu.SMEM)] + [vmem] * len(pieces) + [pl.BlockSpec(memory_space=pl.ANY)],
        out_specs=[vmem] * 2,
        out_shape=[
            jax.ShapeDtypeStruct((tokens, channels), F32),
            jax.ShapeDtypeStruct((channels, channels), BF16),
        ],
        scratch_shapes=[
            pltpu.VMEM((len(pieces), channels, channels), BF16),
            pltpu.SemaphoreType.DMA((ring,)),
        ],
        compiler_params=vmem_limit(48),
    )(index, *pieces, full_weight)
    return pl.pallas_call(
        finish_kernel, out_shape=jax.ShapeDtypeStruct((tokens, channels), BF16), compiler_params=vmem_limit(8)
    )(total, up, down, last_weight)


def solution(mesh):
    placed = (
        P("seq", "tensor"),
        P("seq", "tensor"),
        P("seq", "tensor"),
        P("tensor"),
        P("seq", "tensor"),
    )
    return jax.shard_map(
        body, mesh=mesh, in_specs=placed, out_specs=P("seq", "tensor"), check_vma=False
    )
```

```python
import functools
import math

import jax
import jax.numpy as jnp
import ml_dtypes
import numpy as np
from jax import lax
from jax.experimental import pallas as pl
from jax.experimental.pallas import tpu as pltpu
from jax.sharding import PartitionSpec as P

F32 = jnp.float32
BF16 = jnp.bfloat16
MIB = 1024 * 1024


def split_np(table):
    high = table.astype(ml_dtypes.bfloat16)
    low = (table - high.astype(np.float64)).astype(ml_dtypes.bfloat16)
    return high, low


def phases(left, right, modulus):
    return (left[:, None] * right[None, :] % modulus) * (2.0 * math.pi / modulus)


def dft_tables(blocks, inner):
    outer = 2 * blocks
    length = outer * inner
    freqs = blocks + 1
    held = -(-freqs // 8) * 8
    f = np.arange(freqs)
    b = np.arange(blocks)
    i = np.arange(inner)
    first = np.zeros((2 * held, blocks))
    angle = phases(f, b, outer)
    first[:freqs] = np.cos(angle)
    first[held : held + freqs] = -np.sin(angle)
    turn = np.zeros((2 * held, inner))
    turn[:freqs] = np.cos(phases(f, i, length))
    turn[held : held + freqs] = np.sin(phases(f, i, length))
    angle = phases(i, i, inner)
    mid = np.concatenate([np.cos(angle), np.sin(angle)], axis=1)
    weight = np.where((f == 0) | (f == blocks), 1.0, 2.0) / length
    last = np.zeros((blocks, 2 * held))
    angle = phases(b, f, outer)
    last[:, :freqs] = np.cos(angle) * weight
    last[:, held : held + freqs] = -np.sin(angle) * weight
    last_high, last_low = split_np(last)
    parts = [
        np.concatenate(split_np(mid), axis=0),
        np.concatenate(split_np(turn), axis=1),
        np.concatenate(split_np(first), axis=1),
        np.concatenate([last_high, last_high, last_low], axis=1),
    ]
    width = 2 * inner
    table = np.concatenate([np.pad(part, ((0, 0), (0, width - part.shape[1]))) for part in parts], axis=0)
    ends = np.cumsum([part.shape[0] for part in parts])
    return table, [(int(end) - part.shape[0], int(end), part.shape[1]) for end, part in zip(ends, parts)]


def split(values):
    high = values.astype(BF16)
    low = (values - high.astype(F32)).astype(BF16)
    return high, low


def pack_kernel(signal_ref, taps_ref, out_ref):
    tokens, channels = signal_ref.shape
    sig = signal_ref[...].astype(F32).T.reshape(channels // 8, 8, tokens)
    ker = taps_ref[...].T.reshape(channels // 8, 8, tokens)
    out_ref[...] = jnp.concatenate([sig, ker], axis=1).astype(BF16)


def spread_mid(short, mid):
    inner = short.shape[1] // 2
    for n, rows in enumerate((0, inner)):
        cos, sin = short[rows : rows + inner, :inner], short[rows : rows + inner, inner:]
        mid[2 * n * inner : (2 * n + 1) * inner, :inner] = cos
        mid[2 * n * inner : (2 * n + 1) * inner, inner:] = -sin
        mid[(2 * n + 1) * inner : (2 * n + 2) * inner, :inner] = sin
        mid[(2 * n + 1) * inner : (2 * n + 2) * inner, inner:] = cos


def three_products(cat, mid, rows):
    depth = mid.shape[0] // 2
    product = jnp.dot(cat[:rows, :depth], mid[:depth, :], preferred_element_type=F32)
    product += jnp.dot(cat[:rows, :depth], mid[depth:, :], preferred_element_type=F32)
    return product + jnp.dot(cat[:rows, depth:], mid[:depth, :], preferred_element_type=F32)


def conv_kernel(places, x_ref, table_ref, out_ref, flat, cat, spec, back, mid, turn):
    parts = [table_ref.at[pl.ds(start, end - start), pl.ds(0, width)] for start, end, width in places]
    short_ref, turn_ref, first_ref, last_ref = parts
    held = turn.shape[0] // 2
    spread_mid(short_ref, mid)
    turn[...] = turn_ref[:, : turn.shape[1]].astype(F32) + turn_ref[:, turn.shape[1] :].astype(F32)
    cos_ref, sin_ref = turn.at[pl.ds(0, held)], turn.at[pl.ds(held, held)]
    blocks, rows, inner = x_ref.shape
    chans = rows // 2
    lanes = flat.shape[1]
    halves = inner // lanes
    span = blocks * rows
    for h in range(halves):
        flat[h * span : (h + 1) * span, :] = (
            x_ref[:, :, h * lanes : (h + 1) * lanes].astype(F32).reshape(span, lanes)
        )
    for c in range(chans):
        columns = [
            flat[pl.ds(h * span + row, blocks, stride=rows), :] for row in (c, chans + c) for h in range(halves)
        ]
        x = jnp.concatenate(columns, axis=1).astype(BF16)
        both = jnp.dot(first_ref[...], jnp.concatenate([x, x], axis=0), preferred_element_type=F32)
        parts = []
        for a in (both[:, :inner], both[:, inner:]):
            real, imag = a[:held], a[held:]
            turned = [real * cos_ref[...] + imag * sin_ref[...], imag * cos_ref[...] - real * sin_ref[...]]
            parts.append(jnp.concatenate(turned, axis=1))
        high, low = split(jnp.concatenate(parts, axis=0))
        here = pl.ds(c * 2 * held, 2 * held)
        cat[here, : 2 * inner] = high
        cat[here, 2 * inner :] = low
    spec[...] = three_products(cat, mid, chans * 2 * held)
    for c in range(0, chans, 2):
        parts = []
        for one in (c, c + 1):
            s = spec[pl.ds(one * 2 * held, held), :]
            k = spec[pl.ds(one * 2 * held + held, held), :]
            sr, si, kr, ki = s[:, :inner], s[:, inner:], k[:, :inner], k[:, inner:]
            parts.append(jnp.concatenate([sr * kr - si * ki, -(sr * ki + si * kr)], axis=1))
        high, low = split(jnp.concatenate(parts, axis=0))
        here = pl.ds(c * held, 2 * held)
        cat[here, : 2 * inner] = high
        cat[here, 2 * inner :] = low
    half = chans * held
    spec[:half, :] = three_products(cat, mid, half)
    for c in range(chans):
        q = spec[pl.ds(c * held, held), :]
        qr, qi = q[:, :inner], -q[:, inner:]
        v = jnp.concatenate(
            [qr * cos_ref[...] - qi * sin_ref[...], qr * sin_ref[...] + qi * cos_ref[...]], axis=0
        )
        high, low = split(v)
        y = jnp.dot(last_ref[...], jnp.concatenate([high, low, high], axis=0), preferred_element_type=F32)
        for h in range(inner // lanes):
            back[pl.ds(h * chans + c, blocks, stride=rows), :] = y[:, h * lanes : (h + 1) * lanes]
    out_ref[...] = back[...].reshape(blocks, rows, lanes).astype(BF16)


def gate_kernel(back_ref, signal_ref, gating_ref, skip_ref, out_ref):
    groups, rows, lanes = back_ref.shape
    chans = 8
    tokens, channels = signal_ref.shape
    y = back_ref[...].astype(F32)
    for h in range(tokens // lanes):
        conv = y[:, h * chans : (h + 1) * chans, :].reshape(channels, lanes).T
        here = pl.ds(h * lanes, lanes)
        mixed = conv + skip_ref[...] * signal_ref[here, :].astype(F32)
        out_ref[here, :] = (gating_ref[here, :].astype(F32) * mixed).astype(BF16)


def project_kernel(index_ref, *refs):
    *pieces, w_ref, total_ref, last_ref, held, arrived = refs
    depth = held.shape[1]
    copies = []
    for n in range(len(pieces) + 1):
        rows = pl.ds(pl.multiple_of(index_ref[n] * depth, depth), depth)
        target = held.at[n] if n < len(pieces) else last_ref
        copies.append(pltpu.make_async_copy(w_ref.at[rows, :], target, arrived.at[n]))
        copies[n].start()
    total = None
    for n, piece in enumerate(pieces):
        copies[n].wait()
        product = jnp.dot(piece[...], held[n], preferred_element_type=F32)
        total = product if total is None else total + product
    total_ref[...] = total
    copies[-1].wait()


def finish_kernel(total_ref, up_ref, down_ref, w_ref, out_ref):
    piece = jnp.concatenate([up_ref[...], down_ref[...]], axis=0)
    product = jnp.dot(piece, w_ref[...], preferred_element_type=F32)
    out_ref[...] = (total_ref[...] + product).astype(BF16)


def vmem_limit(mebibytes):
    return pltpu.CompilerParams(vmem_limit_bytes=mebibytes * MIB)


def body(signal, kernel_taps, gating, skip_gain, out_weight):
    seq_count = lax.axis_size("seq")
    ring = lax.axis_size("tensor")
    tokens, channels = signal.shape
    full_weight = lax.all_gather(out_weight, "seq", axis=0, tiled=True)
    table, places = dft_tables(seq_count, tokens)
    turn_rows = places[1][1] - places[1][0]
    held = turn_rows // 2
    vmem = pl.BlockSpec(memory_space=pltpu.VMEM)
    packed = pl.pallas_call(
        pack_kernel,
        out_shape=jax.ShapeDtypeStruct((channels // 8, 16, tokens), BF16),
        compiler_params=vmem_limit(8),
    )(signal, kernel_taps)
    packed, table = lax.optimization_barrier((packed, jnp.asarray(table)))
    spread = lax.all_to_all(packed, "seq", split_axis=0, concat_axis=0, tiled=True)
    convolved = pl.pallas_call(
        functools.partial(conv_kernel, places),
        out_shape=jax.ShapeDtypeStruct((seq_count, 16, 128), BF16),
        scratch_shapes=[
            pltpu.VMEM((tokens // 128 * seq_count * 16, 128), F32),
            pltpu.VMEM((16 * held, 4 * tokens), BF16),
            pltpu.VMEM((16 * held, 2 * tokens), F32),
            pltpu.VMEM((seq_count * 16, 128), F32),
            pltpu.VMEM((4 * tokens, 2 * tokens), BF16),
            pltpu.VMEM((turn_rows, tokens), F32),
        ],
        compiler_params=vmem_limit(24),
    )(spread, table)
    returned = lax.all_to_all(convolved, "seq", split_axis=0, concat_axis=0, tiled=True)
    gated = pl.pallas_call(
        gate_kernel, out_shape=jax.ShapeDtypeStruct((tokens, channels), BF16), compiler_params=vmem_limit(8)
    )(returned, signal, gating, skip_gain.reshape(1, channels))
    up_pairs = [(t, (t + 1) % ring) for t in range(ring)]
    down_pairs = [(t, (t - 1) % ring) for t in range(ring)]
    pieces, offsets = [gated], [0]
    up = down = gated
    for n in range(1, ring // 2):
        up = lax.ppermute(up, "tensor", up_pairs)
        down = lax.ppermute(down, "tensor", down_pairs)
        pieces += [up, down]
        offsets += [-n, n]
    up = lax.ppermute(up[: tokens // 2], "tensor", up_pairs)
    down = lax.ppermute(down[tokens // 2 :], "tensor", down_pairs)
    offsets.append(ring // 2)
    index = (lax.axis_index("tensor") + jnp.asarray(offsets, jnp.int32)) % ring
    total, last_weight = pl.pallas_call(
        project_kernel,
        in_specs=[pl.BlockSpec(memory_space=pltpu.SMEM)] + [vmem] * len(pieces) + [pl.BlockSpec(memory_space=pl.ANY)],
        out_specs=[vmem] * 2,
        out_shape=[
            jax.ShapeDtypeStruct((tokens, channels), F32),
            jax.ShapeDtypeStruct((channels, channels), BF16),
        ],
        scratch_shapes=[
            pltpu.VMEM((len(pieces), channels, channels), BF16),
            pltpu.SemaphoreType.DMA((ring,)),
        ],
        compiler_params=vmem_limit(48),
    )(index, *pieces, full_weight)
    return pl.pallas_call(
        finish_kernel, out_shape=jax.ShapeDtypeStruct((tokens, channels), BF16), compiler_params=vmem_limit(8)
    )(total, up, down, last_weight)


def solution(mesh):
    placed = (
        P("seq", "tensor"),
        P("seq", "tensor"),
        P("seq", "tensor"),
        P("tensor"),
        P("seq", "tensor"),
    )
    return jax.shard_map(
        body, mesh=mesh, in_specs=placed, out_specs=P("seq", "tensor"), check_vma=False
    )
```
